32 devices in a mesh: grp: 2 (over y), region: 4 (over z), batch: 2 (over x), sub: 2 (over core).
Axes of the slice: x: 2, y: 2, z: 4, core: 2. Of those that a mesh axis runs over, the one named last changes fastest.
Arguments:
- params: float32 [8, 640, 128], P(('grp', 'region')), parts along dimension 0
- first_moment: float32 [8, 640, 128], P(('grp', 'region'), ('batch', 'sub')), parts along dimension 0, may hold values from -0.0006 to 0.0006
- second_moment: float32 [8, 640, 128], P(('grp', 'region'), ('batch', 'sub')), parts along dimension 0, may hold values from 1e-09 to 1e-07
- points: float32 [2, 4, 3, 32, 2048], P(None, 'region', None, None, ('grp', 'batch', 'sub')), parts along dimension 4, may hold values from -1 to 1
- deltas: float32 [2, 4, 32, 2048], P(None, 'region', None, ('grp', 'batch', 'sub')), parts along dimension 3, may hold values from 0.03125 to 0.25
- counts: int32 [2, 4, 2048], P(None, 'region', ('grp', 'batch', 'sub')), parts along dimension 2, may hold values from 0 to 32, as said below
- order: int32 [2, 2048, 4], P(None, ('grp', 'batch', 'sub')), parts along dimension 1, may hold values from 0 to 3, each once within a row
- targets: float32 [2, 3, 2048], P(None, None, ('grp', 'batch', 'sub')), parts along dimension 2, may hold values from 0 to 1
Outputs:
- new_params: float32 [8, 640, 128], P(('grp', 'region')), parts along dimension 0
- new_first: float32 [8, 640, 128], P(('grp', 'region'), ('batch', 'sub')), parts along dimension 0
- new_second: float32 [8, 640, 128], P(('grp', 'region'), ('batch', 'sub')), parts along dimension 0
The draws below stay inside these ranges and needn't reach their ends.
There are 2 independent parts, one for each index of `grp`. The reference program is written for one: setup_inputs(seed, part) draws one part's arguments, and reference() takes and returns one part's arrays. A program takes and returns all parts, laid end to end along the dimension named above; each array names one. Nothing has to cross between parts.
Inputs may be any that keep to these rules, and one draw needn't show every extreme that they name: `counts`: every region holds a ray with 32 samples in every step.
All inputs are finite; a program needn't handle non-finite values.
Results may differ from the reference program's by a relative error of at most 0.015.
The reference program's roundings to bfloat16 on the way count: a program that leaves them out, or rounds other values in their place, can miss the bound.
Values sent between devices are 32-bit elements; how exact they have to be, the bound alone decides.
A program may use at most 64 MiB of HBM per device.

```python
import math
import jax
import jax.numpy as jnp
from jax import lax

WIDTH = 256
FREQS = 10
SAMP = 32
STEPS = 2
PROWS = 640
REGIONS = 4
RAYS = 1024


def draw_params(key, part):
    key = jax.random.fold_in(key, 5)
    position = jnp.arange(PROWS * 128).reshape(PROWS, 128)
    first_end = 6 * FREQS * WIDTH
    second_end = first_end + WIDTH * WIDTH
    scaling = jnp.where(position < first_end, math.sqrt(2.0 / (6 * FREQS)), jnp.where(position < second_end, math.sqrt(2.0 / WIDTH), math.sqrt(1.0 / WIDTH)))
    values = jax.random.normal(key, (REGIONS, PROWS, 128), jnp.float32)
    return (values * scaling[None].astype(jnp.float32)).astype(jnp.float32)


def draw_first_moment(key, part):
    key = jax.random.fold_in(key, 7)
    position = jnp.arange(PROWS * 128).reshape(PROWS, 128)
    second_end = 6 * FREQS * WIDTH + WIDTH * WIDTH
    scaling = jnp.where(position < second_end, 1e-06, 0.0002).astype(jnp.float32)
    values = jnp.clip(jax.random.normal(key, (REGIONS, PROWS, 128), jnp.float32), -3.0, 3.0)
    return (values * scaling[None]).astype(jnp.float32)


def draw_counts(key, part):
    key = jax.random.fold_in(key, 11)
    base_key, shift_key = jax.random.split(key)
    base = jax.random.randint(base_key, (STEPS, REGIONS, RAYS), 0, SAMP + 1)
    region_shift = jax.random.randint(shift_key, (STEPS, REGIONS, 1), -(SAMP // 2), SAMP // 2 + 1)
    result = jnp.clip(base + region_shift, 0, SAMP)
    result = result.at[:, :, 0].set(SAMP)
    return result.astype(jnp.int32)


def level_of(own_key, shape, pieces, low, high):
    factor_of = 1.0
    for axis_at, blocks in pieces:
        heights = jax.random.uniform(jax.random.fold_in(jax.random.fold_in(own_key, 6), axis_at), (blocks,), jnp.float32, low / len(pieces), high / len(pieces))
        factor_of = factor_of * jnp.repeat(jnp.exp(heights), shape[axis_at] // blocks).reshape((-1,) + (1,) * (len(shape) - 1 - axis_at))
    return factor_of


def setup_inputs(seed: int = 0, part: int = 0) -> dict:
    arg_keys = jax.random.split(jax.random.key(seed), 9)
    part_splits = jax.random.split(jax.random.fold_in(arg_keys[8], part), 9)
    return {
        "params": draw_params(jax.random.fold_in(jax.random.fold_in(arg_keys[8], part), 71), part),
        "first_moment": draw_first_moment(jax.random.fold_in(jax.random.fold_in(arg_keys[8], part), 71), part),
        "second_moment": jnp.clip(jnp.exp(math.log(1.0000000116860974e-07) - 4.6051702 * jax.random.uniform(part_splits[2], (REGIONS, PROWS, 128), jnp.float32) ** level_of(part_splits[2], (REGIONS, PROWS, 128), ((0, 4), (1, 4)), -0.2, 0.2)), 9.999999717180685e-10, 1.0000000116860974e-07),
        "points": jnp.clip(jax.random.uniform(part_splits[3], (STEPS, REGIONS, 3, SAMP, RAYS), jnp.float32, -1.0, 1.0) * level_of(part_splits[3], (STEPS, REGIONS, 3, SAMP, RAYS), ((1, 4), (4, 4)), -0.4, 0.0), -1.0, 1.0),
        "deltas": jnp.clip(jnp.exp(math.log(0.25) - 2.0794415 * jax.random.uniform(part_splits[4], (STEPS, REGIONS, SAMP, RAYS), jnp.float32) ** level_of(part_splits[4], (STEPS, REGIONS, SAMP, RAYS), ((1, 4), (3, 4)), -0.2, 0.2)), 0.03125, 0.25),
        "counts": draw_counts(jax.random.fold_in(jax.random.fold_in(arg_keys[8], part), 71), part),
        "order": jax.vmap(lambda own: jax.random.permutation(own, REGIONS))(jax.random.split(part_splits[6], STEPS * RAYS)).reshape((STEPS, RAYS, REGIONS)).astype(jnp.int32),
        "targets": jnp.clip(1.0 * jax.random.uniform(part_splits[7], (STEPS, 3, RAYS), jnp.float32) ** level_of(part_splits[7], (STEPS, 3, RAYS), ((2, 4),), -0.2, 0.2), 0.0, 1.0),
    }


BETA_ONE = 0.9
BETA_TWO = 0.999
LEARNING_RATE = 0.02
ADAM_EPSILON = 1e-08

def unpack(weights_flat):
    flattened = weights_flat.reshape(-1)
    first_end = 6 * FREQS * WIDTH
    second_end = first_end + WIDTH * WIDTH
    w_first = flattened[:first_end].reshape(6 * FREQS, WIDTH).astype(jnp.bfloat16)
    w_second = flattened[first_end:second_end].reshape(WIDTH, WIDTH).astype(jnp.bfloat16)
    w_third = flattened[second_end:].reshape(WIDTH, 4).astype(jnp.bfloat16)
    return (w_first, w_second, w_third)

def radiance(weights_flat, sample_points, spacing, live_count):
    samples, ray_count = spacing.shape
    sample_total = samples * ray_count
    frequency = 2.0 ** jnp.arange(FREQS).astype(jnp.float32) * math.pi
    phases = (sample_points[:, None, :, :] * frequency[None, :, None, None]).reshape(3 * FREQS, sample_total)
    encoded = jnp.concatenate([jnp.sin(phases), jnp.cos(phases)], 0).astype(jnp.bfloat16)
    w_first, w_second, w_third = unpack(weights_flat)
    first_act = jax.nn.relu(jnp.dot(w_first.T, encoded, preferred_element_type=jnp.float32)).astype(jnp.bfloat16)
    second_act = jax.nn.relu(jnp.dot(w_second.T, first_act, preferred_element_type=jnp.float32)).astype(jnp.bfloat16)
    network_out = jnp.dot(w_third.T, second_act, preferred_element_type=jnp.float32)
    density = jax.nn.softplus(network_out[0]).reshape(samples, ray_count)
    colour = jax.nn.sigmoid(network_out[1:]).reshape(3, samples, ray_count)
    inside = (lax.broadcasted_iota(jnp.int32, (samples, ray_count), 0) < live_count[None, :]).astype(jnp.float32)
    optical_depth = density * spacing * inside
    depth_sum = lax.optimization_barrier(jnp.sum(optical_depth, 0))
    prior_depth = jnp.cumsum(optical_depth, 0) - optical_depth
    sample_weight = jnp.exp(-prior_depth) * (1.0 - jnp.exp(-optical_depth))
    shaded_colour = lax.optimization_barrier(jnp.sum(sample_weight[None] * colour, 1))
    return (depth_sum, shaded_colour)

def coefficients(depth_sums, colours, depth_ranks, target, rays_total):
    earlier = (depth_ranks[None, :, :] < depth_ranks[:, None, :]).astype(jnp.float32)
    prior_depth = lax.optimization_barrier(jnp.sum(earlier * depth_sums[None, :, :], 1))
    passing = jnp.exp(-prior_depth)
    lighted = passing[:, None, :] * colours
    rendered = lax.optimization_barrier(jnp.sum(lighted, 0))
    pixel_error = 2.0 * (rendered - target) / rays_total
    behind = (depth_ranks[None, :, :] > depth_ranks[:, None, :]).astype(jnp.float32)
    light_after = lax.optimization_barrier(jnp.sum(behind[:, :, None, :] * lighted[None], 1))
    d_depth = -lax.optimization_barrier(jnp.sum(light_after * pixel_error[None], 1))
    d_colour = passing[:, None, :] * pixel_error[None]
    return (d_depth, d_colour)

def forward_items(packed_items):
    return radiance(*packed_items)

def backward_items(packed_items):
    weights_flat, sample_points, spacing, live_count, d_depth, d_colour = packed_items

    def local_field(weights_in):
        return radiance(weights_in, sample_points, spacing, live_count)
    outputs, pullback = jax.vjp(local_field, weights_flat)
    return pullback((d_depth, d_colour))[0]

def reference(params, first_moment, second_moment, points, deltas, counts, order, targets):
    rays_total = float(RAYS)
    for iteration in range(STEPS):
        depth_sums, colours = lax.map(forward_items, (params, points[iteration], deltas[iteration], counts[iteration]))
        depth_ranks = order[iteration].T
        d_depth, d_colour = coefficients(depth_sums, colours, depth_ranks, targets[iteration], rays_total)
        gradient = lax.map(backward_items, (params, points[iteration], deltas[iteration], counts[iteration], d_depth, d_colour))
        first_moment = BETA_ONE * first_moment + (1.0 - BETA_ONE) * gradient
        second_moment = BETA_TWO * second_moment + (1.0 - BETA_TWO) * gradient * gradient
        params = params - LEARNING_RATE * first_moment / (jnp.sqrt(second_moment) + ADAM_EPSILON)
    return (params, first_moment, second_moment)
```

```python
import functools
import math

import jax
import jax.numpy as jnp
from jax import lax
from jax.experimental import pallas as pl
from jax.experimental.pallas import tpu as pltpu
from jax.sharding import PartitionSpec as P

WIDTH = 256
FREQS = 10
HALF = FREQS // 2

BETA_ONE = 0.9
BETA_TWO = 0.999
LEARNING_RATE = 0.02
ADAM_EPSILON = 1e-08

HIGH = lax.Precision.HIGHEST
F32 = jnp.float32
BF16 = jnp.bfloat16
MESH = pl.DeviceIdType.MESH
SLOTS = 4
FIRST = 12 * FREQS
SECOND = FIRST + 2 * WIDTH


def dot(a, b, precision=None):
    return lax.dot_general(
        a, b, (((1,), (0,)), ((), ())), precision=precision, preferred_element_type=F32
    )


def dot_nt(a, b, precision=None):
    return lax.dot_general(
        a, b, (((1,), (1,)), ((), ())), precision=precision, preferred_element_type=F32
    )


def iota(shape, dim):
    return lax.broadcasted_iota(jnp.int32, shape, dim)


def one(mask):
    return jnp.where(mask, 1.0, 0.0).astype(F32)


def sine_cosine(turns):
    turns = turns - 2.0 * jnp.floor(turns * 0.5 + 0.5)
    y = turns * (math.pi / 2)
    z = y * y
    s = -1.0 / 39916800.0
    for coefficient in (1.0 / 362880.0, -1.0 / 5040.0, 1.0 / 120.0, -1.0 / 6.0, 1.0):
        s = s * z + coefficient
    s = s * y
    c = 1.0 / 479001600.0
    for coefficient in (
        -1.0 / 3628800.0,
        1.0 / 40320.0,
        -1.0 / 720.0,
        1.0 / 24.0,
        -0.5,
        1.0,
    ):
        c = c * z + coefficient
    return doubled(s, c)


def doubled(s, c):
    s2 = s + s
    return s2 * c, 1.0 - s2 * s


def kernel(
    steps,
    regions,
    batches,
    subs,
    params_ref,
    first_ref,
    second_ref,
    points_ref,
    deltas_ref,
    counts_ref,
    order_ref,
    targets_ref,
    out_params,
    out_first,
    out_second,
    enc_s,
    h1_s,
    h2_s,
    raw_s,
    dout_s,
    w1_s,
    w1t_s,
    w2_s,
    w2t_s,
    w3_s,
    w3t_s,
    g1_s,
    g2_s,
    g3_s,
    grad_s,
    weights_s,
    gath_s,
    part_s,
    gsend,
    grecv,
    rsend,
    rrecv,
    asend,
    arecv,
):
    samples, rays = deltas_ref.shape[2], deltas_ref.shape[3]
    groups = batches * subs
    shard = first_ref.shape[1]
    rays_total = float(rays * groups)
    region = lax.axis_index("region")
    group = lax.axis_index("batch") * subs + lax.axis_index("sub")
    columns = SLOTS * rays
    chunks = samples // SLOTS
    tiles = rays // 128

    def group_peer(offset):
        peer = lax.rem(group + offset, groups)
        return peer, {"batch": lax.div(peer, subs), "sub": lax.rem(peer, subs)}

    def region_peer(offset):
        return {"region": lax.rem(region + offset, regions)}

    barrier = pltpu.get_barrier_semaphore()
    for offset in range(1, regions):
        pl.semaphore_signal(barrier, inc=1, device_id=region_peer(offset), device_id_type=MESH)
    for offset in range(1, groups):
        pl.semaphore_signal(
            barrier, inc=1, device_id=group_peer(offset)[1], device_id_type=MESH
        )

    dout_s[...] = jnp.zeros_like(dout_s)
    hidden = iota((WIDTH, 128), 0)
    lane = iota((WIDTH, 128), 1)
    third_mask = (lane >> 2) == (hidden & 31)
    spread = one((iota((WIDTH, 8), 0) >> 5) == iota((WIDTH, 8), 1))
    spread_t = one((iota((8, WIDTH), 1) >> 5) == iota((8, WIDTH), 0))
    pick = one((iota((128, 16), 0) & 3) == iota((128, 16), 1))
    pick_t = one((iota((16, 128), 1) & 3) == iota((16, 128), 0))
    eye = one(iota((WIDTH, WIDTH), 0) == iota((WIDTH, WIDTH), 1))
    eye_half = eye.astype(BF16)
    later = one(iota((samples, samples), 0) < iota((samples, samples), 1))
    earlier = one(iota((samples, samples), 0) > iota((samples, samples), 1))

    for step in range(steps):

        def rows_of(start, size, stride):
            if step == 0:
                return params_ref[0, pl.ds(start, size, stride=stride), :]
            return weights_s[step - 1, pl.ds(start, size, stride=stride), :]

        keep = iota((8, 128), 0) < 6
        for kind in range(2):
            for j in range(HALF):
                at = 8 * (kind * HALF + j)
                for side in range(2):
                    block = rows_of(2 * (kind * 3 * FREQS + j) + side, 8, FREQS)
                    w1_s[at : at + 8, side * 128 : (side + 1) * 128] = jnp.where(
                        keep, block, 0.0
                    )
        for side in range(2):
            w2_s[:, side * 128 : (side + 1) * 128] = rows_of(FIRST + side, WIDTH, 2).astype(BF16)
        w1t_s[...] = dot_nt(eye_half, w1_s[...].astype(BF16)).astype(BF16)
        w2t_s[...] = dot_nt(eye_half, w2_s[...]).astype(BF16)
        third = rows_of(SECOND, 8, 1).astype(BF16).astype(F32)
        wide = jnp.where(third_mask, dot(spread, third, HIGH), 0.0)
        w3_s[...] = dot(wide, pick, HIGH).astype(BF16)
        w3t_s[...] = dot_nt(pick_t, wide, HIGH).astype(BF16)

        row = iota((8, rays), 0)
        scaling = jnp.where((row & 1) == 0, 1.0, float(2**HALF))

        def forward(i, carry):
            column = pl.multiple_of(i * columns, columns)
            for s in range(SLOTS):
                t = i * SLOTS + s
                x, y, z = (
                    jnp.broadcast_to(points_ref[step, 0, c, pl.ds(t, 1), :], (8, rays))
                    for c in range(3)
                )
                where = jnp.where(row < 2, x, jnp.where(row < 4, y, z))
                sine, cosine = sine_cosine(where * scaling)
                sines, cosines = [sine], [cosine]
                for _ in range(HALF - 1):
                    sine, cosine = doubled(sine, cosine)
                    sines.append(sine)
                    cosines.append(cosine)
                enc_s[:, pl.ds(pl.multiple_of(column + s * rays, rays), rays)] = jnp.concatenate(
                    sines + cosines, 0
                ).astype(BF16)
            here = pl.ds(column, columns)
            first = jnp.maximum(dot(w1t_s[...], enc_s[:, here]), 0.0).astype(BF16)
            h1_s[:, here] = first
            second = jnp.maximum(dot(w2t_s[...], first), 0.0).astype(BF16)
            h2_s[:, here] = second
            out = dot(w3t_s[...], second)
            for s in range(SLOTS):
                t = i * SLOTS + s
                for k in range(tiles):
                    at = s * rays + k * 128
                    raw_s[k, pl.ds(pl.multiple_of(t * 8, 8), 8), :] = out[:8, at : at + 128]
            return carry

        lax.fori_loop(0, chunks, forward, 0)

        raw = [
            jnp.concatenate(
                [raw_s[k, pl.ds(c, samples, stride=8), :] for k in range(tiles)], 1
            )
            for c in range(4)
        ]
        spacing = jnp.where(
            iota((samples, rays), 0) < counts_ref[step], deltas_ref[step, 0], 0.0
        )
        density = jnp.maximum(raw[0], 0.0) + jnp.log1p(jnp.exp(-jnp.abs(raw[0])))
        optical = density * spacing
        colour = [jax.nn.sigmoid(value) for value in raw[1:]]
        through = jnp.exp(-dot(earlier, optical, HIGH))
        left = jnp.exp(-optical)
        share = through * (1.0 - left)
        summary = [jnp.sum(optical, 0, keepdims=True)]
        summary += [jnp.sum(share * value, 0, keepdims=True) for value in colour]
        gath_s[step, region] = jnp.concatenate(
            summary + [jnp.zeros((4, rays), F32)], 0
        )

        if step == 0:
            pl.semaphore_wait(barrier, regions - 1 + groups - 1)
        copies = []
        for offset in range(1, regions):
            copy = pltpu.make_async_remote_copy(
                src_ref=gath_s.at[step, region],
                dst_ref=gath_s.at[step, region],
                send_sem=gsend.at[step, offset - 1],
                recv_sem=grecv.at[step, offset - 1],
                device_id=region_peer(offset),
                device_id_type=MESH,
            )
            copy.start()
            copies.append(copy)
        slope = [value * (1.0 - value) * share for value in colour]
        density_slope = jax.nn.sigmoid(raw[0]) * spacing
        ranks = dot_nt(
            one(iota((regions, regions), 0) == iota((regions, regions), 1)),
            order_ref[step].astype(F32),
            HIGH,
        )
        g1_s[...] = jnp.zeros_like(g1_s)
        g2_s[...] = jnp.zeros_like(g2_s)
        g3_s[...] = jnp.zeros_like(g3_s)
        for copy in copies:
            copy.wait()

        depths = [gath_s[step, r, 0:1, :] for r in range(regions)]
        rank = [ranks[r : r + 1] for r in range(regions)]
        rendered = [jnp.zeros((1, rays), F32)] * 3
        lighted, passing_own, rank_own = [], jnp.zeros((1, rays), F32), jnp.zeros((1, rays), F32)
        for r in range(regions):
            prior = jnp.zeros((1, rays), F32)
            for q in range(regions):
                if q != r:
                    prior = prior + jnp.where(rank[q] < rank[r], depths[q], 0.0)
            passing = jnp.exp(-prior)
            lights = [passing * gath_s[step, r, c + 1 : c + 2, :] for c in range(3)]
            lighted.append(lights)
            rendered = [a + b for a, b in zip(rendered, lights)]
            passing_own = jnp.where(region == r, passing, passing_own)
            rank_own = jnp.where(region == r, rank[r], rank_own)
        error = [
            2.0 * (rendered[c] - targets_ref[step, c : c + 1, :]) / rays_total for c in range(3)
        ]
        d_depth = jnp.zeros((1, rays), F32)
        for r in range(regions):
            amount = sum(lighted[r][c] * error[c] for c in range(3))
            d_depth = d_depth - jnp.where(rank[r] > rank_own, amount, 0.0)
        d_colour = [passing_own * value for value in error]

        pull = sum(d_colour[c] * colour[c] for c in range(3))
        after = dot(later, pull * share, HIGH)
        d_optical = pull * through * left - after + d_depth
        d_raw = [d_optical * density_slope] + [d_colour[c] * slope[c] for c in range(3)]
        for c in range(4):
            for k in range(tiles):
                dout_s[k, pl.ds(c, samples, stride=16), :] = d_raw[c][
                    :, k * 128 : (k + 1) * 128
                ]

        def backward(i, carry):
            here = pl.ds(pl.multiple_of(i * columns, columns), columns)
            d_out = jnp.concatenate(
                [
                    dout_s[k, pl.ds(pl.multiple_of((i * SLOTS + s) * 16, 16), 16), :]
                    for s in range(SLOTS)
                    for k in range(tiles)
                ],
                1,
            ).astype(BF16)
            second = h2_s[:, here]
            first = h1_s[:, here]
            zero = jnp.zeros((), BF16)
            g3_s[...] += dot_nt(d_out, second)
            d_second = jnp.where(second > zero, dot(w3_s[...], d_out).astype(BF16), zero)
            d_first = jnp.where(first > zero, dot(w2_s[...], d_second).astype(BF16), zero)
            g2_s[...] += dot_nt(first, d_second)
            g1_s[...] += dot_nt(enc_s[:, here], d_first)
            return carry

        lax.fori_loop(0, chunks, backward, 0)

        for kind in range(2):
            for j in range(HALF):
                at = 8 * (kind * HALF + j)
                for side in range(2):
                    grad_s[
                        step, pl.ds(2 * (kind * 3 * FREQS + j) + side, 6, stride=FREQS), :
                    ] = g1_s[at : at + 6, side * 128 : (side + 1) * 128]
        for side in range(2):
            grad_s[step, pl.ds(FIRST + side, WIDTH, stride=2), :] = g2_s[
                :, side * 128 : (side + 1) * 128
            ]
        third_grad = dot(dot_nt(eye, g3_s[...], HIGH), pick_t, HIGH)
        grad_s[step, SECOND : SECOND + 8, :] = dot(
            spread_t, jnp.where(third_mask, third_grad, 0.0), HIGH
        )

        copies = []
        for offset in range(1, groups):
            peer, where = group_peer(offset)
            copy = pltpu.make_async_remote_copy(
                src_ref=grad_s.at[step, pl.ds(pl.multiple_of(peer * shard, 8), shard), :],
                dst_ref=part_s.at[step, offset - 1],
                send_sem=rsend.at[step, offset - 1],
                recv_sem=rrecv.at[step, offset - 1],
                device_id=where,
                device_id_type=MESH,
            )
            copy.start()
            copies.append(copy)
        mine = pl.ds(pl.multiple_of(group * shard, 8), shard)
        gradient = grad_s[step, mine, :]
        for offset, copy in enumerate(copies):
            copy.wait()
            gradient = gradient + part_s[step, offset]
        if step == 0:
            moment_one, moment_two = first_ref[0], second_ref[0]
            current = params_ref[0, mine, :]
        else:
            moment_one, moment_two = out_first[0], out_second[0]
            current = weights_s[step - 1, mine, :]
        moment_one = BETA_ONE * moment_one + (1.0 - BETA_ONE) * gradient
        moment_two = BETA_TWO * moment_two + (1.0 - BETA_TWO) * gradient * gradient
        out_first[0] = moment_one
        out_second[0] = moment_two
        weights_s[step, mine, :] = current - LEARNING_RATE * moment_one / (
            jnp.sqrt(moment_two) + ADAM_EPSILON
        )
        copies = []
        for offset in range(1, groups):
            copy = pltpu.make_async_remote_copy(
                src_ref=weights_s.at[step, mine, :],
                dst_ref=weights_s.at[step, mine, :],
                send_sem=asend.at[step, offset - 1],
                recv_sem=arecv.at[step, offset - 1],
                device_id=group_peer(offset)[1],
                device_id_type=MESH,
            )
            copy.start()
            copies.append(copy)
        for copy in copies:
            copy.wait()
    out_params[0] = weights_s[steps - 1]


def body(params, first_moment, second_moment, points, deltas, counts, order, targets):
    steps, _, _, samples, rays = points.shape
    regions = lax.axis_size("region")
    batches, subs = lax.axis_size("batch"), lax.axis_size("sub")
    groups = batches * subs
    total = samples * rays
    rows, lanes = params.shape[1:]
    shard = first_moment.shape[1]
    dma = pltpu.SemaphoreType.DMA
    vmem = pl.BlockSpec(memory_space=pltpu.VMEM)
    return pl.pallas_call(
        functools.partial(kernel, steps, regions, batches, subs),
        out_shape=(
            jax.ShapeDtypeStruct(params.shape, F32),
            jax.ShapeDtypeStruct(first_moment.shape, F32),
            jax.ShapeDtypeStruct(second_moment.shape, F32),
        ),
        in_specs=[vmem] * 8,
        out_specs=(vmem,) * 3,
        scratch_shapes=[
            pltpu.VMEM((16 * HALF, total), BF16),
            pltpu.VMEM((WIDTH, total), BF16),
            pltpu.VMEM((WIDTH, total), BF16),
            pltpu.VMEM((rays // 128, samples * 8, 128), F32),
            pltpu.VMEM((rays // 128, samples * 16, 128), F32),
            pltpu.VMEM((16 * HALF, WIDTH), F32),
            pltpu.VMEM((WIDTH, 16 * HALF), BF16),
            pltpu.VMEM((WIDTH, WIDTH), BF16),
            pltpu.VMEM((WIDTH, WIDTH), BF16),
            pltpu.VMEM((WIDTH, 16), BF16),
            pltpu.VMEM((16, WIDTH), BF16),
            pltpu.VMEM((16 * HALF, WIDTH), F32),
            pltpu.VMEM((WIDTH, WIDTH), F32),
            pltpu.VMEM((16, WIDTH), F32),
            pltpu.VMEM((steps, rows, lanes), F32),
            pltpu.VMEM((steps, rows, lanes), F32),
            pltpu.VMEM((steps, regions, 8, rays), F32),
            pltpu.VMEM((steps, groups - 1, shard, lanes), F32),
            dma((steps, regions - 1)),
            dma((steps, regions - 1)),
            dma((steps, groups - 1)),
            dma((steps, groups - 1)),
            dma((steps, groups - 1)),
            dma((steps, groups - 1)),
        ],
        compiler_params=pltpu.CompilerParams(
            collective_id=0, has_side_effects=True, vmem_limit_bytes=48 * 1024 * 1024
        ),
    )(params, first_moment, second_moment, points, deltas, counts, order, targets)


def solution(mesh):
    placed = (
        P(("grp", "region"), None, None),
        P(("grp", "region"), ("batch", "sub"), None),
        P(("grp", "region"), ("batch", "sub"), None),
        P(None, "region", None, None, ("grp", "batch", "sub")),
        P(None, "region", None, ("grp", "batch", "sub")),
        P(None, "region", ("grp", "batch", "sub")),
        P(None, ("grp", "batch", "sub"), None),
        P(None, None, ("grp", "batch", "sub")),
    )
    return jax.shard_map(
        body,
        mesh=mesh,
        in_specs=placed,
        out_specs=(
            P(("grp", "region"), None, None),
            P(("grp", "region"), ("batch", "sub"), None),
            P(("grp", "region"), ("batch", "sub"), None),
        ),
        check_vma=False,
    )
```

```python
import functools
import math

import jax
import jax.numpy as jnp
from jax import lax
from jax.experimental import pallas as pl
from jax.experimental.pallas import tpu as pltpu
from jax.sharding import PartitionSpec as P

WIDTH = 256
FREQS = 10
HALF = FREQS // 2

BETA_ONE = 0.9
BETA_TWO = 0.999
LEARNING_RATE = 0.02
ADAM_EPSILON = 1e-08

HIGH = lax.Precision.HIGHEST
F32 = jnp.float32
BF16 = jnp.bfloat16
MESH = pl.DeviceIdType.MESH
SLOTS = 32
FIRST = 12 * FREQS
SECOND = FIRST + 2 * WIDTH


def dot(a, b, precision=None):
    return lax.dot_general(
        a, b, (((1,), (0,)), ((), ())), precision=precision, preferred_element_type=F32
    )


def dot_nt(a, b, precision=None):
    return lax.dot_general(
        a, b, (((1,), (1,)), ((), ())), precision=precision, preferred_element_type=F32
    )


def iota(shape, dim):
    return lax.broadcasted_iota(jnp.int32, shape, dim)


def one(mask):
    return jnp.where(mask, 1.0, 0.0).astype(F32)


def sine_cosine(turns):
    turns = turns - 2.0 * jnp.floor(turns * 0.5 + 0.5)
    y = turns * (math.pi / 2)
    z = y * y
    s = -1.0 / 39916800.0
    for coefficient in (1.0 / 362880.0, -1.0 / 5040.0, 1.0 / 120.0, -1.0 / 6.0, 1.0):
        s = s * z + coefficient
    s = s * y
    c = 1.0 / 479001600.0
    for coefficient in (
        -1.0 / 3628800.0,
        1.0 / 40320.0,
        -1.0 / 720.0,
        1.0 / 24.0,
        -0.5,
        1.0,
    ):
        c = c * z + coefficient
    return doubled(s, c)


def doubled(s, c):
    s2 = s + s
    return s2 * c, 1.0 - s2 * s


def kernel(
    steps,
    regions,
    batches,
    subs,
    params_hbm,
    first_hbm,
    second_hbm,
    points_hbm,
    deltas_hbm,
    counts_ref,
    order_ref,
    targets_ref,
    out_params,
    out_first,
    out_second,
    params_ref,
    first_ref,
    second_ref,
    points_ref,
    deltas_ref,
    enc_s,
    h1_s,
    h2_s,
    raw_s,
    dout_s,
    w1_s,
    w1t_s,
    w2_s,
    w2t_s,
    w3_s,
    w3t_s,
    third_s,
    g1_s,
    g2_s,
    g3_s,
    grad_s,
    weights_s,
    gath_s,
    core_s,
    chip_s,
    part_s,
    loads,
    gsend,
    grecv,
    csend,
    crecv,
    rsend,
    rrecv,
    asend,
    arecv,
    bsend,
    brecv,
):
    samples, rays = deltas_ref.shape[2], deltas_ref.shape[3]
    groups = batches * subs
    shard = first_ref.shape[1]
    rays_total = float(rays * groups)
    region = lax.axis_index("region")
    batch = lax.axis_index("batch")
    sub = lax.axis_index("sub")
    columns = SLOTS * 128
    chunks = samples // SLOTS
    parts = rays // 128

    fetches = []
    for k, (source, target) in enumerate(
        (
            (points_hbm, points_ref),
            (params_hbm, params_ref),
            (deltas_hbm, deltas_ref),
            (first_hbm, first_ref),
            (second_hbm, second_ref),
        )
    ):
        fetch = pltpu.make_async_copy(source, target, loads.at[k])
        fetch.start()
        fetches.append(fetch)

    def region_peer(offset):
        return {"region": lax.rem(region + offset, regions)}

    def batch_peer(offset):
        return {"batch": lax.rem(batch + offset, batches)}

    def sub_peer(offset):
        return {"sub": lax.rem(sub + offset, subs)}

    def shard_rows(batch_at, sub_at):
        return pl.ds(pl.multiple_of((batch_at * subs + sub_at) * shard, 8), shard)

    def send(source, target, send_sem, recv_sem, where):
        copy = pltpu.make_async_remote_copy(
            src_ref=source,
            dst_ref=target,
            send_sem=send_sem,
            recv_sem=recv_sem,
            device_id=where,
            device_id_type=MESH,
        )
        copy.start()
        return copy

    barrier = pltpu.get_barrier_semaphore()
    for count, peer in ((regions, region_peer), (batches, batch_peer), (subs, sub_peer)):
        for offset in range(1, count):
            pl.semaphore_signal(
                barrier, inc=1, device_id=peer(offset), device_id_type=MESH
            )

    dout_s[...] = jnp.zeros_like(dout_s)
    flat = iota((4 * WIDTH, 128), 0)
    lane = iota((4 * WIDTH, 128), 1)
    third_s[...] = one(
        ((flat & 31) == (lane >> 2)) & ((flat >> 8) == (lane & 3))
    ).astype(BF16)
    third_mask = ((iota((8, 4 * WIDTH), 1) & (WIDTH - 1)) >> 5) == iota((8, 4 * WIDTH), 0)
    eye_half = one(iota((WIDTH, WIDTH), 0) == iota((WIDTH, WIDTH), 1)).astype(BF16)
    later = one(iota((samples, samples), 0) < iota((samples, samples), 1))
    earlier = one(iota((samples, samples), 0) > iota((samples, samples), 1))
    row = iota((8, 128), 0)
    scaling = jnp.where((row & 1) == 0, 1.0, float(2**HALF))
    keep = row < 6

    def encode(step, part):
        def chunk(i, carry):
            blocks = [
                points_ref[
                    step,
                    0,
                    c,
                    pl.ds(pl.multiple_of(i * SLOTS, SLOTS), SLOTS),
                    part * 128 : (part + 1) * 128,
                ]
                for c in range(3)
            ]
            for s in range(SLOTS):
                t = i * SLOTS + s
                x, y, z = (
                    jnp.broadcast_to(block[s : s + 1], (8, 128)) for block in blocks
                )
                where = jnp.where(row < 2, x, jnp.where(row < 4, y, z))
                sine, cosine = sine_cosine(where * scaling)
                sines, cosines = [sine], [cosine]
                for _ in range(HALF - 1):
                    sine, cosine = doubled(sine, cosine)
                    sines.append(sine)
                    cosines.append(cosine)
                at = pl.multiple_of(part * samples * 128 + t * 128, 128)
                enc_s[step, :, pl.ds(at, 128)] = jnp.concatenate(sines + cosines, 0).astype(
                    BF16
                )
            return carry

        lax.fori_loop(0, chunks, chunk, 0)

    fetches[0].wait()
    for part in range(parts):
        encode(0, part)
    fetches[1].wait()

    for step in range(steps):

        def rows_of(start, size, stride):
            if step == 0:
                return params_ref[0, pl.ds(start, size, stride=stride), :]
            return weights_s[step - 1, pl.ds(start, size, stride=stride), :]

        for kind in range(2):
            for j in range(HALF):
                at = 8 * (kind * HALF + j)
                for side in range(2):
                    block = rows_of(2 * (kind * 3 * FREQS + j) + side, 8, FREQS)
                    w1_s[at : at + 8, side * 128 : (side + 1) * 128] = jnp.where(
                        keep, block, 0.0
                    )
        for side in range(2):
            w2_s[:, side * 128 : (side + 1) * 128] = rows_of(FIRST + side, WIDTH, 2).astype(BF16)
        w1t_s[...] = dot_nt(eye_half, w1_s[...].astype(BF16)).astype(BF16)
        w2t_s[...] = dot_nt(eye_half, w2_s[...]).astype(BF16)
        third = jnp.concatenate([rows_of(SECOND, 8, 1), jnp.zeros((8, 128), F32)], 0)
        wide = dot_nt(third.astype(BF16), third_s[...])[:8]
        wide = jnp.sum(jnp.where(third_mask, wide, 0.0), 0, keepdims=True)
        w3t_s[...] = jnp.concatenate(
            [wide[:, c * WIDTH : (c + 1) * WIDTH] for c in range(4)]
            + [jnp.zeros((12, WIDTH), F32)],
            0,
        ).astype(BF16)
        w3_s[...] = dot_nt(eye_half, w3t_s[...]).astype(BF16)
        g1_s[...] = jnp.zeros_like(g1_s)
        g2_s[...] = jnp.zeros_like(g2_s)
        g3_s[...] = jnp.zeros_like(g3_s)

        kept, exchanges = [], []
        for part in range(parts):
            base = part * samples * 128
            own = slice(part * 128, (part + 1) * 128)

            def forward(i, carry):
                here = pl.ds(pl.multiple_of(base + i * columns, columns), columns)
                first = jnp.maximum(dot(w1t_s[...], enc_s[step, :, here]), 0.0).astype(BF16)
                h1_s[:, here] = first
                second = jnp.maximum(dot(w2t_s[...], first), 0.0).astype(BF16)
                h2_s[:, here] = second
                out = dot(w3t_s[...], second)
                for s in range(SLOTS):
                    raw_s[part, pl.ds(pl.multiple_of((i * SLOTS + s) * 8, 8), 8), :] = out[
                        :8, s * 128 : (s + 1) * 128
                    ]
                return carry

            lax.fori_loop(0, chunks, forward, 0)

            if step == 0 and part == 0:
                fetches[2].wait()
            raw = [raw_s[part, pl.ds(c, samples, stride=8), :] for c in range(4)]
            spacing = jnp.where(
                iota((samples, 128), 0) < counts_ref[step, :, own],
                deltas_ref[step, 0, :, own],
                0.0,
            )
            density = jnp.maximum(raw[0], 0.0) + jnp.log1p(jnp.exp(-jnp.abs(raw[0])))
            optical = density * spacing
            colour = [jax.nn.sigmoid(value) for value in raw[1:]]
            through = jnp.exp(-dot(earlier, optical, HIGH))
            left = jnp.exp(-optical)
            share = through * (1.0 - left)
            summary = [jnp.sum(optical, 0, keepdims=True)]
            summary += [jnp.sum(share * value, 0, keepdims=True) for value in colour]
            gath_s[step, part, region] = jnp.concatenate(
                summary + [jnp.zeros((4, 128), F32)], 0
            )
            if step == 0 and part == 0:
                pl.semaphore_wait(barrier, regions + batches + subs - 3)
            mine = gath_s.at[step, part, region]
            exchanges.append(
                [
                    send(
                        mine,
                        mine,
                        gsend.at[step, part, offset - 1],
                        grecv.at[step, part, offset - 1],
                        region_peer(offset),
                    )
                    for offset in range(1, regions)
                ]
            )
            slope = [value * (1.0 - value) * share for value in colour]
            kept.append(
                (colour, share, through * left, slope, jax.nn.sigmoid(raw[0]) * spacing)
            )

        for part in range(parts):
            base = part * samples * 128
            own = slice(part * 128, (part + 1) * 128)
            colour, share, remain, slope, density_slope = kept[part]
            for copy in exchanges[part]:
                copy.wait()

            rank = [order_ref[step, r : r + 1, own] for r in range(regions)]
            depths = [gath_s[step, part, r, 0:1, :] for r in range(regions)]
            rendered = [jnp.zeros((1, 128), F32)] * 3
            lighted = []
            passing_own, rank_own = jnp.zeros((1, 128), F32), jnp.zeros((1, 128), jnp.int32)
            for r in range(regions):
                prior = jnp.zeros((1, 128), F32)
                for q in range(regions):
                    if q != r:
                        prior = prior + jnp.where(rank[q] < rank[r], depths[q], 0.0)
                passing = jnp.exp(-prior)
                lights = [passing * gath_s[step, part, r, c + 1 : c + 2, :] for c in range(3)]
                lighted.append(lights)
                rendered = [a + b for a, b in zip(rendered, lights)]
                passing_own = jnp.where(region == r, passing, passing_own)
                rank_own = jnp.where(region == r, rank[r], rank_own)
            error = [
                2.0 * (rendered[c] - targets_ref[c, step : step + 1, own]) / rays_total
                for c in range(3)
            ]
            d_depth = jnp.zeros((1, 128), F32)
            for r in range(regions):
                amount = sum(lighted[r][c] * error[c] for c in range(3))
                d_depth = d_depth - jnp.where(rank[r] > rank_own, amount, 0.0)
            d_colour = [passing_own * value for value in error]

            pull = sum(d_colour[c] * colour[c] for c in range(3))
            after = dot(later, pull * share, HIGH)
            d_optical = pull * remain - after + d_depth
            dout_s[part, pl.ds(0, samples, stride=16), :] = d_optical * density_slope
            for c in range(3):
                dout_s[part, pl.ds(c + 1, samples, stride=16), :] = d_colour[c] * slope[c]

            def backward(i, carry):
                here = pl.ds(pl.multiple_of(base + i * columns, columns), columns)
                d_out = jnp.concatenate(
                    [
                        dout_s[part, pl.ds(pl.multiple_of((i * SLOTS + s) * 16, 16), 16), :]
                        for s in range(SLOTS)
                    ],
                    1,
                ).astype(BF16)
                second = h2_s[:, here]
                first = h1_s[:, here]
                zero = jnp.zeros((), BF16)
                g3_s[...] += dot_nt(d_out, second)
                d_second = jnp.where(second > zero, dot(w3_s[...], d_out).astype(BF16), zero)
                d_first = jnp.where(first > zero, dot(w2_s[...], d_second).astype(BF16), zero)
                g2_s[...] += dot_nt(first, d_second)
                g1_s[...] += dot_nt(enc_s[step, :, here], d_first)
                return carry

            lax.fori_loop(0, chunks, backward, 0)

        for kind in range(2):
            for j in range(HALF):
                at = 8 * (kind * HALF + j)
                for side in range(2):
                    grad_s[
                        step, pl.ds(2 * (kind * 3 * FREQS + j) + side, 6, stride=FREQS), :
                    ] = g1_s[at : at + 6, side * 128 : (side + 1) * 128]
        for side in range(2):
            grad_s[step, pl.ds(FIRST + side, WIDTH, stride=2), :] = g2_s[
                :, side * 128 : (side + 1) * 128
            ]
        wide = jnp.concatenate(
            [jnp.broadcast_to(g3_s[c : c + 1, :], (8, WIDTH)) for c in range(4)], 1
        )
        wide = jnp.where(third_mask, wide, 0.0)
        high = wide.astype(BF16).astype(F32)
        middle = (wide - high).astype(BF16).astype(F32)
        low = wide - high - middle
        moved = dot(
            jnp.concatenate([high, middle, low, jnp.zeros_like(low)], 0).astype(BF16),
            third_s[...],
        )
        grad_s[step, SECOND : SECOND + 8, :] = moved[:8] + moved[8:16] + moved[16:24]

        inner = []
        for away in [*range(1, batches), 0]:
            at = lax.rem(batch + away, batches)
            inner.append(
                [
                    send(
                        grad_s.at[step, shard_rows(at, lax.rem(sub + offset, subs)), :],
                        core_s.at[step, away, offset - 1],
                        csend.at[step, away, offset - 1],
                        crecv.at[step, away, offset - 1],
                        sub_peer(offset),
                    )
                    for offset in range(1, subs)
                ]
            )
        outer = []
        for away, copies in zip([*range(1, batches), 0], inner):
            gradient = grad_s[step, shard_rows(lax.rem(batch + away, batches), sub), :]
            for offset, copy in enumerate(copies):
                copy.wait()
                gradient = gradient + core_s[step, away, offset]
            if away:
                chip_s[step, away - 1] = gradient
                outer.append(
                    send(
                        chip_s.at[step, away - 1],
                        part_s.at[step, away - 1],
                        rsend.at[step, away - 1],
                        rrecv.at[step, away - 1],
                        batch_peer(away),
                    )
                )
        if step + 1 < steps:
            for part in range(parts):
                encode(step + 1, part)
        for away, copy in enumerate(outer):
            copy.wait()
            gradient = gradient + part_s[step, away]
        mine = shard_rows(batch, sub)
        if step == 0:
            fetches[3].wait()
            fetches[4].wait()
            moment_one, moment_two = first_ref[0], second_ref[0]
            current = params_ref[0, mine, :]
        else:
            moment_one, moment_two = out_first[0], out_second[0]
            current = weights_s[step - 1, mine, :]
        moment_one = BETA_ONE * moment_one + (1.0 - BETA_ONE) * gradient
        moment_two = BETA_TWO * moment_two + (1.0 - BETA_TWO) * gradient * gradient
        weights_s[step, mine, :] = current - LEARNING_RATE * moment_one / (
            jnp.sqrt(moment_two) + ADAM_EPSILON
        )
        own = weights_s.at[step, mine, :]
        outer = [
            send(
                own, own, asend.at[step, away - 1], arecv.at[step, away - 1], batch_peer(away)
            )
            for away in range(1, batches)
        ]
        out_first[0] = moment_one
        out_second[0] = moment_two
        inner = []
        for away in range(batches):
            if away:
                outer[away - 1].wait()
            got = weights_s.at[step, shard_rows(lax.rem(batch + batches - away, batches), sub), :]
            inner += [
                send(
                    got,
                    got,
                    bsend.at[step, away, offset - 1],
                    brecv.at[step, away, offset - 1],
                    sub_peer(offset),
                )
                for offset in range(1, subs)
            ]
        for copy in inner:
            copy.wait()
    out_params[0] = weights_s[steps - 1]


def body(params, first_moment, second_moment, points, deltas, counts, order, targets):
    steps, _, _, samples, rays = points.shape
    regions = lax.axis_size("region")
    batches, subs = lax.axis_size("batch"), lax.axis_size("sub")
    total = samples * rays
    parts = rays // 128
    rows, lanes = params.shape[1:]
    shard = first_moment.shape[1]
    dma = pltpu.SemaphoreType.DMA
    vmem = pl.BlockSpec(memory_space=pltpu.VMEM)
    hbm = pl.BlockSpec(memory_space=pltpu.HBM)
    return pl.pallas_call(
        functools.partial(kernel, steps, regions, batches, subs),
        out_shape=(
            jax.ShapeDtypeStruct(params.shape, F32),
            jax.ShapeDtypeStruct(first_moment.shape, F32),
            jax.ShapeDtypeStruct(second_moment.shape, F32),
        ),
        in_specs=[hbm] * 5 + [vmem] * 3,
        out_specs=(vmem,) * 3,
        scratch_shapes=[
            *(
                pltpu.VMEM(x.shape, F32)
                for x in (params, first_moment, second_moment, points, deltas)
            ),
            pltpu.VMEM((steps, 16 * HALF, total), BF16),
            pltpu.VMEM((WIDTH, total), BF16),
            pltpu.VMEM((WIDTH, total), BF16),
            pltpu.VMEM((parts, samples * 8, 128), F32),
            pltpu.VMEM((parts, samples * 16, 128), F32),
            pltpu.VMEM((16 * HALF, WIDTH), F32),
            pltpu.VMEM((WIDTH, 16 * HALF), BF16),
            pltpu.VMEM((WIDTH, WIDTH), BF16),
            pltpu.VMEM((WIDTH, WIDTH), BF16),
            pltpu.VMEM((WIDTH, 16), BF16),
            pltpu.VMEM((16, WIDTH), BF16),
            pltpu.VMEM((4 * WIDTH, 128), BF16),
            pltpu.VMEM((16 * HALF, WIDTH), F32),
            pltpu.VMEM((WIDTH, WIDTH), F32),
            pltpu.VMEM((16, WIDTH), F32),
            pltpu.VMEM((steps, rows, lanes), F32),
            pltpu.VMEM((steps, rows, lanes), F32),
            pltpu.VMEM((steps, parts, regions, 8, 128), F32),
            pltpu.VMEM((steps, batches, subs - 1, shard, lanes), F32),
            pltpu.VMEM((steps, batches - 1, shard, lanes), F32),
            pltpu.VMEM((steps, batches - 1, shard, lanes), F32),
            dma((5,)),
            dma((steps, parts, regions - 1)),
            dma((steps, parts, regions - 1)),
            dma((steps, batches, subs - 1)),
            dma((steps, batches, subs - 1)),
            dma((steps, batches - 1)),
            dma((steps, batches - 1)),
            dma((steps, batches - 1)),
            dma((steps, batches - 1)),
            dma((steps, batches, subs - 1)),
            dma((steps, batches, subs - 1)),
        ],
        compiler_params=pltpu.CompilerParams(
            collective_id=0, has_side_effects=True, vmem_limit_bytes=48 * 1024 * 1024
        ),
    )(
        params,
        first_moment,
        second_moment,
        points,
        deltas,
        counts,
        jnp.transpose(order, (0, 2, 1)),
        jnp.transpose(targets, (1, 0, 2)),
    )


def solution(mesh):
    placed = (
        P(("grp", "region"), None, None),
        P(("grp", "region"), ("batch", "sub"), None),
        P(("grp", "region"), ("batch", "sub"), None),
        P(None, "region", None, None, ("grp", "batch", "sub")),
        P(None, "region", None, ("grp", "batch", "sub")),
        P(None, "region", ("grp", "batch", "sub")),
        P(None, ("grp", "batch", "sub"), None),
        P(None, None, ("grp", "batch", "sub")),
    )
    return jax.shard_map(
        body,
        mesh=mesh,
        in_specs=placed,
        out_specs=(
            P(("grp", "region"), None, None),
            P(("grp", "region"), ("batch", "sub"), None),
            P(("grp", "region"), ("batch", "sub"), None),
        ),
        check_vma=False,
    )
```

```python
import functools
import math

import jax
import jax.numpy as jnp
from jax import lax
from jax.experimental import pallas as pl
from jax.experimental.pallas import tpu as pltpu
from jax.sharding import PartitionSpec as P

WIDTH = 256
FREQS = 10
HALF = FREQS // 2

BETA_ONE = 0.9
BETA_TWO = 0.999
LEARNING_RATE = 0.02
ADAM_EPSILON = 1e-08

HIGH = lax.Precision.HIGHEST
F32 = jnp.float32
BF16 = jnp.bfloat16
MESH = pl.DeviceIdType.MESH
SLOTS = 32
FIRST = 12 * FREQS
SECOND = FIRST + 2 * WIDTH


def dot(a, b, precision=None):
    return lax.dot_general(
        a, b, (((1,), (0,)), ((), ())), precision=precision, preferred_element_type=F32
    )


def dot_nt(a, b, precision=None):
    return lax.dot_general(
        a, b, (((1,), (1,)), ((), ())), precision=precision, preferred_element_type=F32
    )


def aligned(index, multiple):
    return index if isinstance(index, int) else pl.multiple_of(index, multiple)


def repeat(count, step):
    if count == 1:
        step(0, 0)
    else:
        lax.fori_loop(0, count, step, 0)


def iota(shape, dim):
    return lax.broadcasted_iota(jnp.int32, shape, dim)


def one(mask):
    return jnp.where(mask, 1.0, 0.0).astype(F32)


def sine_cosine(turns):
    turns = turns - 2.0 * jnp.floor(turns * 0.5 + 0.5)
    y = turns * (math.pi / 2)
    z = y * y
    s = -1.0 / 39916800.0
    for coefficient in (1.0 / 362880.0, -1.0 / 5040.0, 1.0 / 120.0, -1.0 / 6.0, 1.0):
        s = s * z + coefficient
    s = s * y
    c = 1.0 / 479001600.0
    for coefficient in (
        -1.0 / 3628800.0,
        1.0 / 40320.0,
        -1.0 / 720.0,
        1.0 / 24.0,
        -0.5,
        1.0,
    ):
        c = c * z + coefficient
    return doubled(s, c)


def doubled(s, c):
    s2 = s + s
    return s2 * c, 1.0 - s2 * s


def kernel(
    steps,
    regions,
    batches,
    subs,
    params_hbm,
    first_hbm,
    second_hbm,
    points_hbm,
    deltas_hbm,
    counts_ref,
    order_ref,
    targets_ref,
    out_params,
    out_first,
    out_second,
    params_ref,
    first_ref,
    second_ref,
    points_ref,
    deltas_ref,
    enc_s,
    h1_s,
    h2_s,
    raw_s,
    dout_s,
    w1_s,
    w1t_s,
    w2_s,
    w2t_s,
    w3_s,
    w3t_s,
    third_s,
    g1_s,
    g2_s,
    g3_s,
    grad_s,
    weights_s,
    gath_s,
    core_s,
    chip_s,
    part_s,
    loads,
    gsend,
    grecv,
    csend,
    crecv,
    rsend,
    rrecv,
    asend,
    arecv,
    bsend,
    brecv,
):
    samples, rays = deltas_ref.shape[2], deltas_ref.shape[3]
    groups = batches * subs
    shard = first_ref.shape[1]
    rays_total = float(rays * groups)
    region = lax.axis_index("region")
    batch = lax.axis_index("batch")
    sub = lax.axis_index("sub")
    columns = SLOTS * 128
    chunks = samples // SLOTS
    parts = rays // 128

    fetches = []
    for k, (source, target) in enumerate(
        (
            (points_hbm, points_ref),
            (params_hbm, params_ref),
            (deltas_hbm, deltas_ref),
            (first_hbm, first_ref),
            (second_hbm, second_ref),
        )
    ):
        fetch = pltpu.make_async_copy(source, target, loads.at[k])
        fetch.start()
        fetches.append(fetch)

    def region_peer(offset):
        return {"region": lax.rem(region + offset, regions)}

    def batch_peer(offset):
        return {"batch": lax.rem(batch + offset, batches)}

    def sub_peer(offset):
        return {"sub": lax.rem(sub + offset, subs)}

    def shard_rows(batch_at, sub_at):
        return pl.ds(aligned((batch_at * subs + sub_at) * shard, 8), shard)

    def send(source, target, send_sem, recv_sem, where):
        copy = pltpu.make_async_remote_copy(
            src_ref=source,
            dst_ref=target,
            send_sem=send_sem,
            recv_sem=recv_sem,
            device_id=where,
            device_id_type=MESH,
        )
        copy.start()
        return copy

    barrier = pltpu.get_barrier_semaphore()
    for count, peer in ((regions, region_peer), (batches, batch_peer), (subs, sub_peer)):
        for offset in range(1, count):
            pl.semaphore_signal(
                barrier, inc=1, device_id=peer(offset), device_id_type=MESH
            )

    dout_s[...] = jnp.zeros_like(dout_s)
    flat = iota((4 * WIDTH, 128), 0)
    lane = iota((4 * WIDTH, 128), 1)
    third_s[...] = one(
        ((flat & 31) == (lane >> 2)) & ((flat >> 8) == (lane & 3))
    ).astype(BF16)
    third_mask = ((iota((8, 4 * WIDTH), 1) & (WIDTH - 1)) >> 5) == iota((8, 4 * WIDTH), 0)
    eye_half = one(iota((WIDTH, WIDTH), 0) == iota((WIDTH, WIDTH), 1)).astype(BF16)
    later = one(iota((samples, samples), 0) < iota((samples, samples), 1))
    earlier = one(iota((samples, samples), 0) > iota((samples, samples), 1))
    row = iota((8, 128), 0)
    scaling = jnp.where((row & 1) == 0, 1.0, float(2**HALF))
    keep = row < 6

    def encode(step, part):
        def chunk(i, carry):
            blocks = [
                points_ref[
                    step,
                    0,
                    c,
                    pl.ds(aligned(i * SLOTS, SLOTS), SLOTS),
                    part * 128 : (part + 1) * 128,
                ]
                for c in range(3)
            ]
            for s in range(SLOTS):
                t = i * SLOTS + s
                x, y, z = (
                    jnp.broadcast_to(block[s : s + 1], (8, 128)) for block in blocks
                )
                where = jnp.where(row < 2, x, jnp.where(row < 4, y, z))
                sine, cosine = sine_cosine(where * scaling)
                sines, cosines = [sine], [cosine]
                for _ in range(HALF - 1):
                    sine, cosine = doubled(sine, cosine)
                    sines.append(sine)
                    cosines.append(cosine)
                at = aligned(part * samples * 128 + t * 128, 128)
                enc_s[step, :, pl.ds(at, 128)] = jnp.concatenate(sines + cosines, 0).astype(
                    BF16
                )
            return carry

        repeat(chunks, chunk)

    fetches[0].wait()
    fetches[1].wait()
    for part in range(parts):
        encode(0, part)

    for step in range(steps):

        def rows_of(start, size, stride):
            if step == 0:
                return params_ref[0, pl.ds(start, size, stride=stride), :]
            return weights_s[step - 1, pl.ds(start, size, stride=stride), :]

        for kind in range(2):
            for j in range(HALF):
                at = 8 * (kind * HALF + j)
                for side in range(2):
                    block = rows_of(2 * (kind * 3 * FREQS + j) + side, 8, FREQS)
                    w1_s[at : at + 8, side * 128 : (side + 1) * 128] = jnp.where(
                        keep, block, 0.0
                    )
        for side in range(2):
            w2_s[:, side * 128 : (side + 1) * 128] = rows_of(FIRST + side, WIDTH, 2).astype(BF16)
        w1t_s[...] = dot_nt(eye_half, w1_s[...].astype(BF16)).astype(BF16)
        w2t_s[...] = dot_nt(eye_half, w2_s[...]).astype(BF16)
        third = jnp.concatenate([rows_of(SECOND, 8, 1), jnp.zeros((8, 128), F32)], 0)
        wide = dot_nt(third.astype(BF16), third_s[...])[:8]
        wide = jnp.sum(jnp.where(third_mask, wide, 0.0), 0, keepdims=True)
        w3t_s[...] = jnp.concatenate(
            [wide[:, c * WIDTH : (c + 1) * WIDTH] for c in range(4)]
            + [jnp.zeros((12, WIDTH), F32)],
            0,
        ).astype(BF16)
        w3_s[...] = dot_nt(eye_half, w3t_s[...]).astype(BF16)
        g1_s[...] = jnp.zeros_like(g1_s)
        g2_s[...] = jnp.zeros_like(g2_s)
        g3_s[...] = jnp.zeros_like(g3_s)

        kept, exchanges = [], []
        for part in range(parts):
            base = part * samples * 128
            own = slice(part * 128, (part + 1) * 128)

            def forward(i, carry):
                here = pl.ds(aligned(base + i * columns, columns), columns)
                first = jnp.maximum(dot(w1t_s[...], enc_s[step, :, here]), 0.0).astype(BF16)
                h1_s[:, here] = first
                second = jnp.maximum(dot(w2t_s[...], first), 0.0).astype(BF16)
                h2_s[:, here] = second
                out = dot(w3t_s[...], second)
                for s in range(SLOTS):
                    raw_s[part, pl.ds(aligned((i * SLOTS + s) * 8, 8), 8), :] = out[
                        :8, s * 128 : (s + 1) * 128
                    ]
                return carry

            repeat(chunks, forward)

            if step == 0 and part == 0:
                fetches[2].wait()
            raw = [raw_s[part, pl.ds(c, samples, stride=8), :] for c in range(4)]
            spacing = jnp.where(
                iota((samples, 128), 0) < counts_ref[step, :, own],
                deltas_ref[step, 0, :, own],
                0.0,
            )
            density = jnp.maximum(raw[0], 0.0) + jnp.log1p(jnp.exp(-jnp.abs(raw[0])))
            optical = density * spacing
            colour = [jax.nn.sigmoid(value) for value in raw[1:]]
            through = jnp.exp(-dot(earlier, optical, HIGH))
            left = jnp.exp(-optical)
            share = through * (1.0 - left)
            summary = [jnp.sum(optical, 0, keepdims=True)]
            summary += [jnp.sum(share * value, 0, keepdims=True) for value in colour]
            gath_s[step, part, region] = jnp.concatenate(
                summary + [jnp.zeros((4, 128), F32)], 0
            )
            if step == 0 and part == 0:
                pl.semaphore_wait(barrier, regions + batches + subs - 3)
            mine = gath_s.at[step, part, region]
            exchanges.append(
                [
                    send(
                        mine,
                        mine,
                        gsend.at[step, part, offset - 1],
                        grecv.at[step, part, offset - 1],
                        region_peer(offset),
                    )
                    for offset in range(1, regions)
                ]
            )
            slope = [value * (1.0 - value) * share for value in colour]
            kept.append(
                (colour, share, through * left, slope, jax.nn.sigmoid(raw[0]) * spacing)
            )

        for part in range(parts):
            base = part * samples * 128
            own = slice(part * 128, (part + 1) * 128)
            colour, share, remain, slope, density_slope = kept[part]
            for copy in exchanges[part]:
                copy.wait()

            rank = [order_ref[step, r : r + 1, own] for r in range(regions)]
            depths = [gath_s[step, part, r, 0:1, :] for r in range(regions)]
            rendered = [jnp.zeros((1, 128), F32)] * 3
            lighted = []
            passing_own, rank_own = jnp.zeros((1, 128), F32), jnp.zeros((1, 128), jnp.int32)
            for r in range(regions):
                prior = jnp.zeros((1, 128), F32)
                for q in range(regions):
                    if q != r:
                        prior = prior + jnp.where(rank[q] < rank[r], depths[q], 0.0)
                passing = jnp.exp(-prior)
                lights = [passing * gath_s[step, part, r, c + 1 : c + 2, :] for c in range(3)]
                lighted.append(lights)
                rendered = [a + b for a, b in zip(rendered, lights)]
                passing_own = jnp.where(region == r, passing, passing_own)
                rank_own = jnp.where(region == r, rank[r], rank_own)
            error = [
                2.0 * (rendered[c] - targets_ref[c, step : step + 1, own]) / rays_total
                for c in range(3)
            ]
            d_depth = jnp.zeros((1, 128), F32)
            for r in range(regions):
                amount = sum(lighted[r][c] * error[c] for c in range(3))
                d_depth = d_depth - jnp.where(rank[r] > rank_own, amount, 0.0)
            d_colour = [passing_own * value for value in error]

            pull = sum(d_colour[c] * colour[c] for c in range(3))
            after = dot(later, pull * share, HIGH)
            d_optical = pull * remain - after + d_depth
            dout_s[part, pl.ds(0, samples, stride=16), :] = d_optical * density_slope
            for c in range(3):
                dout_s[part, pl.ds(c + 1, samples, stride=16), :] = d_colour[c] * slope[c]

            def backward(i, carry):
                here = pl.ds(aligned(base + i * columns, columns), columns)
                d_out = jnp.concatenate(
                    [
                        dout_s[part, pl.ds(aligned((i * SLOTS + s) * 16, 16), 16), :]
                        for s in range(SLOTS)
                    ],
                    1,
                ).astype(BF16)
                second = h2_s[:, here]
                first = h1_s[:, here]
                zero = jnp.zeros((), BF16)
                g3_s[...] += dot_nt(d_out, second)
                d_second = jnp.where(second > zero, dot(w3_s[...], d_out).astype(BF16), zero)
                d_first = jnp.where(first > zero, dot(w2_s[...], d_second).astype(BF16), zero)
                g2_s[...] += dot_nt(first, d_second)
                g1_s[...] += dot_nt(enc_s[step, :, here], d_first)
                return carry

            repeat(chunks, backward)

        for kind in range(2):
            for j in range(HALF):
                at = 8 * (kind * HALF + j)
                for side in range(2):
                    grad_s[
                        step, pl.ds(2 * (kind * 3 * FREQS + j) + side, 6, stride=FREQS), :
                    ] = g1_s[at : at + 6, side * 128 : (side + 1) * 128]
        for side in range(2):
            grad_s[step, pl.ds(FIRST + side, WIDTH, stride=2), :] = g2_s[
                :, side * 128 : (side + 1) * 128
            ]
        wide = jnp.concatenate(
            [jnp.broadcast_to(g3_s[c : c + 1, :], (8, WIDTH)) for c in range(4)], 1
        )
        wide = jnp.where(third_mask, wide, 0.0)
        high = wide.astype(BF16).astype(F32)
        middle = (wide - high).astype(BF16).astype(F32)
        low = wide - high - middle
        moved = dot(
            jnp.concatenate([high, middle, low, jnp.zeros_like(low)], 0).astype(BF16),
            third_s[...],
        )
        grad_s[step, SECOND : SECOND + 8, :] = moved[:8] + moved[8:16] + moved[16:24]

        inner = []
        for away in [*range(1, batches), 0]:
            at = lax.rem(batch + away, batches)
            inner.append(
                [
                    send(
                        grad_s.at[step, shard_rows(at, lax.rem(sub + offset, subs)), :],
                        core_s.at[step, away, offset - 1],
                        csend.at[step, away, offset - 1],
                        crecv.at[step, away, offset - 1],
                        sub_peer(offset),
                    )
                    for offset in range(1, subs)
                ]
            )
        outer = []
        for away, copies in zip([*range(1, batches), 0], inner):
            gradient = grad_s[step, shard_rows(lax.rem(batch + away, batches), sub), :]
            for offset, copy in enumerate(copies):
                copy.wait()
                gradient = gradient + core_s[step, away, offset]
            if away:
                chip_s[step, away - 1] = gradient
                outer.append(
                    send(
                        chip_s.at[step, away - 1],
                        part_s.at[step, away - 1],
                        rsend.at[step, away - 1],
                        rrecv.at[step, away - 1],
                        batch_peer(away),
                    )
                )
        if step + 1 < steps:
            for part in range(parts):
                encode(step + 1, part)
        for away, copy in enumerate(outer):
            copy.wait()
            gradient = gradient + part_s[step, away]
        mine = shard_rows(batch, sub)
        if step == 0:
            fetches[3].wait()
            fetches[4].wait()
            moment_one, moment_two = first_ref[0], second_ref[0]
            current = params_ref[0, mine, :]
        else:
            moment_one, moment_two = out_first[0], out_second[0]
            current = weights_s[step - 1, mine, :]
        moment_one = BETA_ONE * moment_one + (1.0 - BETA_ONE) * gradient
        moment_two = BETA_TWO * moment_two + (1.0 - BETA_TWO) * gradient * gradient
        weights_s[step, mine, :] = current - LEARNING_RATE * moment_one / (
            jnp.sqrt(moment_two) + ADAM_EPSILON
        )
        own = weights_s.at[step, mine, :]
        outer = [
            send(
                own, own, asend.at[step, away - 1], arecv.at[step, away - 1], batch_peer(away)
            )
            for away in range(1, batches)
        ]
        out_first[0] = moment_one
        out_second[0] = moment_two
        inner = []
        for away in range(batches):
            if away:
                outer[away - 1].wait()
            got = weights_s.at[step, shard_rows(lax.rem(batch + batches - away, batches), sub), :]
            inner += [
                send(
                    got,
                    got,
                    bsend.at[step, away, offset - 1],
                    brecv.at[step, away, offset - 1],
                    sub_peer(offset),
                )
                for offset in range(1, subs)
            ]
        for copy in inner:
            copy.wait()
    out_params[0] = weights_s[steps - 1]


def body(params, first_moment, second_moment, points, deltas, counts, order, targets):
    steps, _, _, samples, rays = points.shape
    regions = lax.axis_size("region")
    batches, subs = lax.axis_size("batch"), lax.axis_size("sub")
    total = samples * rays
    parts = rays // 128
    rows, lanes = params.shape[1:]
    shard = first_moment.shape[1]
    dma = pltpu.SemaphoreType.DMA
    vmem = pl.BlockSpec(memory_space=pltpu.VMEM)
    hbm = pl.BlockSpec(memory_space=pltpu.HBM)
    return pl.pallas_call(
        functools.partial(kernel, steps, regions, batches, subs),
        out_shape=(
            jax.ShapeDtypeStruct(params.shape, F32),
            jax.ShapeDtypeStruct(first_moment.shape, F32),
            jax.ShapeDtypeStruct(second_moment.shape, F32),
        ),
        in_specs=[hbm] * 5 + [vmem] * 3,
        out_specs=(vmem,) * 3,
        scratch_shapes=[
            *(
                pltpu.VMEM(x.shape, F32)
                for x in (params, first_moment, second_moment, points, deltas)
            ),
            pltpu.VMEM((steps, 16 * HALF, total), BF16),
            pltpu.VMEM((WIDTH, total), BF16),
            pltpu.VMEM((WIDTH, total), BF16),
            pltpu.VMEM((parts, samples * 8, 128), F32),
            pltpu.VMEM((parts, samples * 16, 128), F32),
            pltpu.VMEM((16 * HALF, WIDTH), F32),
            pltpu.VMEM((WIDTH, 16 * HALF), BF16),
            pltpu.VMEM((WIDTH, WIDTH), BF16),
            pltpu.VMEM((WIDTH, WIDTH), BF16),
            pltpu.VMEM((WIDTH, 16), BF16),
            pltpu.VMEM((16, WIDTH), BF16),
            pltpu.VMEM((4 * WIDTH, 128), BF16),
            pltpu.VMEM((16 * HALF, WIDTH), F32),
            pltpu.VMEM((WIDTH, WIDTH), F32),
            pltpu.VMEM((16, WIDTH), F32),
            pltpu.VMEM((steps, rows, lanes), F32),
            pltpu.VMEM((steps, rows, lanes), F32),
            pltpu.VMEM((steps, parts, regions, 8, 128), F32),
            pltpu.VMEM((steps, batches, subs - 1, shard, lanes), F32),
            pltpu.VMEM((steps, batches - 1, shard, lanes), F32),
            pltpu.VMEM((steps, batches - 1, shard, lanes), F32),
            dma((5,)),
            dma((steps, parts, regions - 1)),
            dma((steps, parts, regions - 1)),
            dma((steps, batches, subs - 1)),
            dma((steps, batches, subs - 1)),
            dma((steps, batches - 1)),
            dma((steps, batches - 1)),
            dma((steps, batches - 1)),
            dma((steps, batches - 1)),
            dma((steps, batches, subs - 1)),
            dma((steps, batches, subs - 1)),
        ],
        compiler_params=pltpu.CompilerParams(
            collective_id=0, has_side_effects=True, vmem_limit_bytes=48 * 1024 * 1024
        ),
    )(
        params,
        first_moment,
        second_moment,
        points,
        deltas,
        counts,
        jnp.transpose(order, (0, 2, 1)),
        jnp.transpose(targets, (1, 0, 2)),
    )


def solution(mesh):
    placed = (
        P(("grp", "region"), None, None),
        P(("grp", "region"), ("batch", "sub"), None),
        P(("grp", "region"), ("batch", "sub"), None),
        P(None, "region", None, None, ("grp", "batch", "sub")),
        P(None, "region", None, ("grp", "batch", "sub")),
        P(None, "region", ("grp", "batch", "sub")),
        P(None, ("grp", "batch", "sub"), None),
        P(None, None, ("grp", "batch", "sub")),
    )
    return jax.shard_map(
        body,
        mesh=mesh,
        in_specs=placed,
        out_specs=(
            P(("grp", "region"), None, None),
            P(("grp", "region"), ("batch", "sub"), None),
            P(("grp", "region"), ("batch", "sub"), None),
        ),
        check_vma=False,
    )
```
